128 devices in a mesh: img: 8 (over z, core), txt: 16 (over x, y).
Axes of the slice: x: 4, y: 4, z: 4, core: 2. Of those that a mesh axis runs over, the one named last changes fastest.
Arguments:
- teacher_image: bfloat16 [16384, 1280], P(('img', 'txt')), may hold values from -24 to 24
- teacher_text: bfloat16 [16384, 1280], P(('txt', 'img')), may hold values from -24 to 24
- student_image: bfloat16 [16384, 512], P(('img', 'txt')), may hold values from -24 to 24
- student_text: bfloat16 [16384, 512], P(('txt', 'img')), may hold values from -24 to 24
Outputs:
- loss: float32 [], replicated
- image_grad: float32 [16384, 512], P(('img', 'txt'))
- text_grad: float32 [16384, 512], P(('txt', 'img'))
The draws below stay inside these ranges and needn't reach their ends.
All inputs are finite; a program needn't handle non-finite values.
Results may differ from the reference program's by a relative error of at most 0.0012.
Values may be sent and summed in bfloat16 or wider, within the bound.
A program may use at most 128 MiB of HBM per device.

```python
import math
import jax
import jax.numpy as jnp
from jax import lax

TWIDTH = 1280
SWIDTH = 512
PAIRS = 16384


def pair_rows(key, side, ramp):
    key = jax.random.fold_in(key, 11 + side)
    key_normal = jax.random.fold_in(key, 0)
    key_scale = jax.random.fold_in(key, 2)
    key_extra = jax.random.fold_in(key, 3)
    normal_part = jax.random.truncated_normal(key_normal, -4.0, 4.0, (PAIRS, TWIDTH), jnp.float32)
    field = normal_part
    position = jnp.arange(PAIRS, dtype=jnp.float32) / PAIRS
    spread = jnp.exp(jax.random.uniform(key_scale, (PAIRS, 1), jnp.float32, math.log(0.5), math.log(1.6)))
    scales = spread * (1.0 + ramp * position)[:, None]
    extra = jax.random.truncated_normal(key_extra, -4.0, 4.0, (PAIRS, SWIDTH), jnp.float32)
    return (field * scales, scales * (0.8 * field[:, :SWIDTH] + 0.6 * extra))


def draw_teacher_image(key, part):
    teacher_rows, student_rows = pair_rows(key, 0, 0.5)
    return teacher_rows.astype(jnp.bfloat16)


def draw_student_image(key, part):
    teacher_rows, student_rows = pair_rows(key, 0, 0.5)
    return student_rows.astype(jnp.bfloat16)


def draw_teacher_text(key, part):
    teacher_rows, student_rows = pair_rows(key, 1, 0.5)
    return teacher_rows.astype(jnp.bfloat16)


def draw_student_text(key, part):
    teacher_rows, student_rows = pair_rows(key, 1, 0.5)
    return student_rows.astype(jnp.bfloat16)


def setup_inputs(seed: int = 0) -> dict:
    splits = jax.random.split(jax.random.key(seed), 5)
    teacher_image = draw_teacher_image(jax.random.fold_in(splits[4], 71), 0)
    teacher_text = draw_teacher_text(jax.random.fold_in(splits[4], 71), 0)
    student_image = draw_student_image(jax.random.fold_in(splits[4], 71), 0)
    student_text = draw_student_text(jax.random.fold_in(splits[4], 71), 0)
    return dict(teacher_image=teacher_image, teacher_text=teacher_text, student_image=student_image, student_text=student_text)


def both_logits(image_teacher, image_student, text_teacher, text_student):
    teacher_logit = jnp.dot(image_teacher, text_teacher.T, preferred_element_type=jnp.float32) * (TWIDTH ** -0.5)
    student_logit = jnp.dot(image_student, text_student.T, preferred_element_type=jnp.float32) * (SWIDTH ** -0.5)
    return teacher_logit, student_logit


def row_logsumexp(logit):
    highest = jnp.max(logit, axis=1)
    return highest + jnp.log(jnp.sum(jnp.exp(logit - highest[:, None]), axis=1))


def fold_columns(column_peak, column_total, logit):
    new_peak = jnp.maximum(column_peak, jnp.max(logit, axis=0))
    new_total = column_total * jnp.exp(column_peak - new_peak) + jnp.sum(jnp.exp(logit - new_peak[None, :]), axis=0)
    return new_peak, new_total


def split_delta(delta):
    delta_high = delta.astype(jnp.bfloat16)
    widened = lax.optimization_barrier(delta_high).astype(jnp.float32)
    delta_low = (delta - widened).astype(jnp.bfloat16)
    return delta_high, delta_low


def reference(teacher_image, teacher_text, student_image, student_text):
    block_rows = min(1024, PAIRS)
    blocks = PAIRS // block_rows
    image_teacher = teacher_image.reshape(blocks, block_rows, TWIDTH)
    image_student = student_image.reshape(blocks, block_rows, SWIDTH)

    def gather_stats(running, pieces):
        peak_teacher, total_teacher, peak_student, total_student = running
        teacher_logit, student_logit = both_logits(pieces[0], pieces[1], teacher_text, student_text)
        peak_teacher, total_teacher = fold_columns(peak_teacher, total_teacher, teacher_logit)
        peak_student, total_student = fold_columns(peak_student, total_student, student_logit)
        return (peak_teacher, total_teacher, peak_student, total_student), (row_logsumexp(teacher_logit), row_logsumexp(student_logit))

    empty_peak = jnp.full((PAIRS,), -jnp.inf, jnp.float32)
    empty_total = jnp.zeros((PAIRS,), jnp.float32)
    running, row_parts = lax.scan(gather_stats, (empty_peak, empty_total, empty_peak, empty_total), (image_teacher, image_student))
    teacher_column_lse = running[0] + jnp.log(running[1])
    student_column_lse = running[2] + jnp.log(running[3])
    teacher_row_lse = row_parts[0].reshape(PAIRS)
    student_row_lse = row_parts[1].reshape(PAIRS)

    def gradient_pass(running, pieces):
        text_total, divergence = running
        block_teacher, block_student, lse_teacher, lse_student = pieces
        teacher_logit, student_logit = both_logits(block_teacher, block_student, teacher_text, student_text)
        teacher_row_prob = jnp.exp(teacher_logit - lse_teacher[:, None])
        student_row_prob = jnp.exp(student_logit - lse_student[:, None])
        teacher_column_prob = jnp.exp(teacher_logit - teacher_column_lse[None, :])
        student_column_prob = jnp.exp(student_logit - student_column_lse[None, :])
        difference = teacher_logit - student_logit
        divergence = divergence + jnp.sum(teacher_row_prob * difference) + jnp.sum(teacher_column_prob * difference)
        delta = (student_row_prob - teacher_row_prob) + (student_column_prob - teacher_column_prob)
        delta_high, delta_low = split_delta(delta)
        image_part = jnp.dot(delta_high, student_text, preferred_element_type=jnp.float32) + jnp.dot(delta_low, student_text, preferred_element_type=jnp.float32)
        text_total = text_total + jnp.dot(delta_high.T, block_student, preferred_element_type=jnp.float32) + jnp.dot(delta_low.T, block_student, preferred_element_type=jnp.float32)
        return (text_total, divergence), image_part

    start = (jnp.zeros((PAIRS, SWIDTH), jnp.float32), jnp.zeros((), jnp.float32))
    finished, image_parts = lax.scan(gradient_pass, start, (image_teacher, image_student, teacher_row_lse.reshape(blocks, block_rows), student_row_lse.reshape(blocks, block_rows)))
    text_total, divergence = finished
    total = divergence + jnp.sum(student_row_lse - teacher_row_lse) + jnp.sum(student_column_lse - teacher_column_lse)
    loss = total / (2.0 * PAIRS)
    image_grad = image_parts.reshape(PAIRS, SWIDTH) * (SWIDTH ** -0.5)
    text_grad = text_total * (SWIDTH ** -0.5)
    return loss, image_grad, text_grad
```

```python
import functools
import math

import jax
import jax.numpy as jnp
from jax import lax
from jax.experimental import pallas as pl
from jax.experimental.pallas import tpu as pltpu
from jax.sharding import PartitionSpec as P

MESH = pl.DeviceIdType.MESH
F32 = jnp.float32
BF16 = jnp.bfloat16
UNIT = 128
TW = 1280
SW = 512
W = TW + SW
NI = 8
NP = 8
FIRST = 5
LOG2E = 1.4426950408889634
LN2 = 0.6931471805599453
LOW = -1e30
CODE = 2.0**18
TINY = 1e-25


def inv(k):
    return (k // 4) * 4 + (4 - k % 4) % 4


def dot_nt(a, b):
    return lax.dot_general(a, b, (((1,), (1,)), ((), ())), preferred_element_type=F32)


def encode(v):
    v2 = v * v
    return (v2 * v2 * v).astype(BF16)


def decode(code):
    y = code.astype(F32)
    u = jnp.exp2(jnp.log2(jnp.abs(y)) * 0.2)
    return jnp.where(y < 0.0, -u, u)


def log_sum(peak, total):
    return peak + jnp.log2(total)


def kernel(
    pairs,
    ti, tt, si, st,
    loss_o, ig_o, tg_o,
    img, txt, lt, ls, rm, rs, cm, cs, d, ist,
    rmsg, cmsg, rrx, crx, rlse, clse,
    isend, irecv, xsend, xrecv, keep, tsend, trecv,
    lsend, lrx_i, lrx_t,
    lsem, ssem, rsem,
):
    i_index, t_index = lax.axis_index("img"), lax.axis_index("txt")
    z, c, x, y = i_index // 2, i_index % 2, t_index // 4, t_index % 4
    xa = x + 1 - 2 * (x % 2)
    xb = 3 - x

    def i_peer(k):
        return (z * 2 + c, (xa if k // 4 else x) * 4 + (y + k % 4) % 4)

    def t_peer(cc, k):
        return (((z + k % 4) % 4) * 2 + (c + cc) % 2, (xb if k // 4 else x) * 4 + y)

    serial = [0]
    begun = []

    def send(src, dst, device):
        n = serial[0]
        serial[0] += 1
        copy = pltpu.make_async_remote_copy(
            src_ref=src, dst_ref=dst, send_sem=ssem.at[n], recv_sem=rsem.at[n],
            device_id=device, device_id_type=MESH,
        )
        copy.start()
        begun.append(copy)
        return copy

    loads = [
        pltpu.make_async_copy(ti, img.at[0, :, 0:TW], lsem.at[0]),
        pltpu.make_async_copy(si, img.at[0, :, TW:W], lsem.at[1]),
        pltpu.make_async_copy(tt, txt.at[0, :, 0:TW], lsem.at[2]),
        pltpu.make_async_copy(st, txt.at[0, :, TW:W], lsem.at[3]),
    ]
    for copy in loads:
        copy.start()
    barrier = pltpu.get_barrier_semaphore()
    for k in range(1, 8):
        pl.semaphore_signal(barrier, inc=1, device_id=i_peer(k), device_id_type=MESH)
    for j in range(1, 16):
        pl.semaphore_signal(barrier, inc=1, device_id=t_peer(j % 2, j // 2), device_id_type=MESH)
    rm[...] = jnp.full(rm.shape, LOW, F32)
    rs[...] = jnp.zeros(rs.shape, F32)
    cm[...] = jnp.full(cm.shape, LOW, F32)
    cs[...] = jnp.zeros(cs.shape, F32)
    pl.semaphore_wait(barrier, 22)
    for copy in loads:
        copy.wait()

    def image_at(k, half=None):
        return img.at[k] if half is None else img.at[k, pl.ds(half * 64, 64)]

    def text_at(k, half=None):
        return txt.at[2 * k] if half is None else txt.at[2 * k, pl.ds(half * 64, 64)]

    sides = ((image_at, i_peer, False), (text_at, functools.partial(t_peer, 0), True))
    crossings = []

    def cross(k):
        crossings.append(send(txt.at[2 * k], txt.at[2 * k + 1], t_peer(1, 0)))

    flight = []
    for at, peer, _ in sides:
        flight.append(
            dict(
                plus=send(at(0), at(3), peer(1)),
                minus=send(at(0), at(1), peer(3)),
                side=send(at(0), at(4), peer(4)),
            )
        )
    cross(0)
    for (at, peer, is_text), f in zip(sides, flight):
        f["minus"].wait_recv()
        f["far_minus"] = send(at(1, 0), at(2, 0), peer(3))
        f["plus"].wait_recv()
        f["far_plus"] = send(at(3, 1), at(2, 1), peer(1))
        if is_text:
            cross(1)
            cross(3)
    for (at, peer, is_text), f in zip(sides, flight):
        f["side"].wait_recv()
        f["side_plus"] = send(at(4), at(7), peer(1))
        f["side_minus"] = send(at(4), at(5), peer(3))
        if is_text:
            cross(4)
    for (at, peer, is_text), f in zip(sides, flight):
        f["far_minus"].wait_recv()
        f["far_plus"].wait_recv()
        f["side_far"] = send(at(2), at(6), peer(4))
        if is_text:
            cross(2)
    for copy in crossings:
        copy.wait_recv()
    crossings.clear()

    scale_t = LOG2E * TW**-0.5
    scale_s = LOG2E * SW**-0.5

    def fold(model, logit, p, u):
        rows = pl.ds(u * UNIT, UNIT)
        left, right = logit[p, rows, 0:128], logit[p, rows, 128:256]
        old = rm[model, rows, :]
        new = jnp.maximum(old, jnp.maximum(left, right))
        rm[model, rows, :] = new
        rs[model, rows, :] = (
            rs[model, rows, :] * jnp.exp2(old - new) + jnp.exp2(left - new) + jnp.exp2(right - new)
        )
        for h, part in ((0, left), (1, right)):
            lanes = slice(h * 128, h * 128 + 128)
            part = part.reshape(16, 8, 128)
            old = cm[model, p, :, lanes]
            new = jnp.maximum(old, jnp.max(part, axis=0))
            cm[model, p, :, lanes] = new
            cs[model, p, :, lanes] = cs[model, p, :, lanes] * jnp.exp2(old - new) + jnp.sum(
                jnp.exp2(part - new[None]), axis=0
            )

    def block(p, u0, count):
        rows = slice(u0 * UNIT, (u0 + count) * UNIT)
        both = pl.ds(p * 2, 2)
        lt[p, rows, :] = scale_t * dot_nt(
            img[u0 : u0 + count, :, 0:TW].reshape(count * UNIT, TW),
            txt[both, :, 0:TW].reshape(2 * UNIT, TW),
        )
        ls[p, rows, :] = scale_s * dot_nt(
            img[u0 : u0 + count, :, TW:W].reshape(count * UNIT, SW),
            txt[both, :, TW:W].reshape(2 * UNIT, SW),
        )

        @pl.loop(u0, u0 + count)
        def _(u):
            fold(0, lt, p, u)
            fold(1, ls, p, u)

    @pl.loop(0, FIRST)
    def _(p):
        block(p, 0, FIRST)

    for (at, peer, is_text), f in zip(sides, flight):
        f["side_plus"].wait_recv()
        f["side_minus"].wait_recv()
        if is_text:
            cross(5)
            cross(7)
        f["side_far"].wait_recv()
        if is_text:
            cross(6)
    for copy in crossings:
        copy.wait_recv()

    @pl.loop(0, FIRST)
    def _(p):
        block(p, FIRST, NI - FIRST)

    @pl.loop(FIRST, NP)
    def _(p):
        block(p, 0, 4)
        block(p, 4, 4)

    def largest(ref, count):
        def step(n, best):
            part = jnp.abs(ref[n, :, TW:W].astype(F32)).reshape(16, 8, SW)
            return jnp.maximum(best, jnp.max(part, axis=0))

        best = lax.fori_loop(0, count, step, jnp.zeros((8, SW), F32))
        return jnp.broadcast_to(jnp.max(best, axis=(0, 1), keepdims=True), (1, 128))

    image_top = jnp.maximum(largest(img, NI), TINY)
    text_top = jnp.maximum(largest(txt, 2 * NP), TINY)

    @pl.loop(0, NI)
    def _(u):
        rows = pl.ds(pl.multiple_of(u * UNIT, UNIT), UNIT)
        for model in range(2):
            peaks = rm[model, rows, :].T
            totals = rs[model, rows, :].T
            peak = jnp.max(peaks, axis=0, keepdims=True)
            total = jnp.sum(totals * jnp.exp2(peaks - peak), axis=0, keepdims=True)
            rmsg[u, model : model + 1, :] = log_sum(peak, total)
        rmsg[u, 2:8, :] = jnp.zeros((6, 128), F32)

    @pl.loop(0, NP)
    def _(p):
        for model in range(2):
            peaks = cm[model, p]
            peak = jnp.max(peaks, axis=0, keepdims=True)
            total = jnp.sum(cs[model, p] * jnp.exp2(peaks - peak), axis=0, keepdims=True)
            lse = log_sum(peak, total)
            for h in range(2):
                cmsg[2 * p + h, model : model + 1, :] = lse[:, h * 128 : h * 128 + 128]
        for h in range(2):
            cmsg[2 * p + h, 2:3, :] = image_top
            cmsg[2 * p + h, 3:8, :] = jnp.zeros((5, 128), F32)

    parts = [send(rmsg.at[k], rrx.at[inv(k)], i_peer(k)) for k in range(1, 8)]
    parts += [
        send(cmsg.at[j], crx.at[2 * inv(j // 2) + j % 2], t_peer(j % 2, j // 2))
        for j in range(1, 16)
    ]
    for block_index in range(NI // 2):
        turned = img[2 * block_index : 2 * block_index + 2, :, TW:W].reshape(2 * UNIT, SW).T
        ist[:, block_index * 512 : block_index * 512 + 256] = turned
        ist[:, block_index * 512 + 256 : block_index * 512 + 512] = turned
    for copy in parts:
        copy.wait_recv()

    def combine(own, received, count):
        peak = own
        for k in range(1, count):
            peak = jnp.maximum(peak, received[k])
        total = jnp.exp2(own - peak)
        for k in range(1, count):
            total = total + jnp.exp2(received[k] - peak)
        return log_sum(peak, total)

    chip_top = jnp.maximum(image_top, crx[1, 2:3, :])
    rlse[0] = combine(rmsg[0], rrx, 8)
    rlse[0, 2:3, :] = text_top
    clse[0] = combine(cmsg[0], crx, 16)
    clse[0, 2:3, :] = chip_top
    parts = [send(rlse.at[0], rlse.at[inv(k)], i_peer(k)) for k in range(1, 8)]
    parts += [
        send(clse.at[0], clse.at[2 * inv(j // 2) + j % 2], t_peer(j % 2, j // 2))
        for j in range(1, 16)
    ]
    gap = (rlse[0, 1:2, :] - rlse[0, 0:1, :]) + (clse[0, 1:2, :] - clse[0, 0:1, :])
    for copy in parts:
        copy.wait_recv()

    image_code = CODE * SW**-0.5 / text_top[0:1, 0:1]
    text_code = CODE * SW**-0.5 / chip_top[0:1, 0:1]
    grad_flights = []
    diverge = jnp.zeros((8, 128), F32)
    for b in (3, 1, 2, 0):
        rows = slice(b * 256, b * 256 + 256)
        lse_t, lse_s = (
            jnp.concatenate(
                [
                    jnp.broadcast_to(rlse[2 * b + h, model : model + 1, :], (128, 128)).T
                    for h in range(2)
                ],
                axis=0,
            )
            for model in range(2)
        )

        def step(p, carry, b=b, rows=rows, lse_t=lse_t, lse_s=lse_s):
            total, diverge = carry
            for h in range(2):
                lanes = slice(h * 128, h * 128 + 128)
                t = lt[p, rows, lanes]
                s = ls[p, rows, lanes]
                j = 2 * p + h
                teacher = jnp.exp2(t - lse_t) + jnp.exp2(t - clse[j, 0:1, :])
                student = jnp.exp2(s - lse_s) + jnp.exp2(s - clse[j, 1:2, :])
                diverge = diverge + jnp.sum((teacher * (t - s)).reshape(32, 8, 128), axis=0)
                delta = student - teacher
                high = delta.astype(BF16)
                low = (delta - high.astype(F32)).astype(BF16)
                d[p, b, 0:256, lanes] = high
                d[p, b, 256:512, lanes] = low
            weights = txt[pl.ds(2 * p, 2), :, TW:W].reshape(2 * UNIT, SW)
            total = total + jnp.dot(d[p, b], weights, preferred_element_type=F32)
            return total, diverge

        total, diverge = lax.fori_loop(0, NP, step, (jnp.zeros((512, SW), F32), diverge))
        total = total[0:256] + total[256:512]
        for h in (1, 0):
            k = 2 * b + h
            part = total[h * 128 : h * 128 + 128]
            if k == 0:
                ig_o[...] = part * SW**-0.5
            else:
                isend[k] = encode(part * image_code)
                grad_flights.append(send(isend.at[k], irecv.at[inv(k)], i_peer(k)))

    first_row = lax.broadcasted_iota(jnp.int32, (8, 128), 0) == 0
    lsend[0] = diverge + jnp.where(first_row, jnp.broadcast_to(gap, (8, 128)), 0.0)
    loss_flights = [send(lsend.at[0], lrx_i.at[inv(k)], i_peer(k)) for k in range(1, 8)]

    order = [6, 5, 7, 2, 1, 3, 4, 0]
    crossed = []

    def pass_on(k):
        crossed[order.index(k)].wait_recv()
        part = keep[k] + xrecv[k]
        if k == 0:
            keep[0] = part
        else:
            tsend[k] = encode(part * text_code)
            grad_flights.append(send(tsend.at[k], trecv.at[inv(k)], t_peer(0, k)))

    for n, k in enumerate(order):
        part = jnp.dot(ist[...], d[k].reshape(2048, 256), preferred_element_type=F32)
        keep[k] = part[:, 0:128]
        xsend[k] = part[:, 128:256]
        crossed.append(send(xsend.at[k], xrecv.at[k], t_peer(1, 0)))
        if n >= 1:
            pass_on(order[n - 1])
        if n == 4:
            for copy in loss_flights:
                copy.wait_recv()
            loss_part = lsend[0]
            for q in range(1, 8):
                loss_part = loss_part + lrx_i[q]
            lsend[1] = loss_part
            loss_flights = [
                send(lsend.at[1], lrx_t.at[2 * inv(j // 2) + j % 2], t_peer(j % 2, j // 2))
                for j in range(1, 16)
            ]
    pass_on(order[-1])

    for copy in loss_flights:
        copy.wait_recv()
    loss_part = lsend[1]
    for q in range(1, 16):
        loss_part = loss_part + lrx_t[q]
    loss = jnp.sum(loss_part, axis=(0, 1), keepdims=True) * (LN2 / (2.0 * pairs))
    loss_o[...] = jnp.broadcast_to(loss, (8, 128))

    for copy in grad_flights:
        copy.wait_recv()
    image_total = ig_o[...]
    for k in range(1, 8):
        image_total = image_total + decode(irecv[k]) * (rlse[k, 2:3, 0:1] * (1.0 / CODE))
    ig_o[...] = image_total
    text_total = keep[0] * SW**-0.5
    for k in range(1, 8):
        text_total = text_total + decode(trecv[k]) * (clse[2 * k, 2:3, 0:1] * (1.0 / CODE))
    tg_o[...] = text_total.T
    for copy in begun:
        copy.wait_send()


def local(teacher_image, teacher_text, student_image, student_text):
    pairs = teacher_image.shape[0] * lax.axis_size("img") * lax.axis_size("txt")
    vmem = pltpu.VMEM
    loss, image_grad, text_grad = pl.pallas_call(
        functools.partial(kernel, pairs),
        out_shape=(
            jax.ShapeDtypeStruct((8, 128), F32),
            jax.ShapeDtypeStruct((UNIT, SW), F32),
            jax.ShapeDtypeStruct((UNIT, SW), F32),
        ),
        in_specs=[pl.BlockSpec(memory_space=pl.ANY)] * 4,
        out_specs=[pl.BlockSpec(memory_space=vmem)] * 3,
        scratch_shapes=[
            vmem((NI, UNIT, W), BF16),
            vmem((2 * NP, UNIT, W), BF16),
            vmem((NP, NI * UNIT, 256), F32),
            vmem((NP, NI * UNIT, 256), F32),
            vmem((2, NI * UNIT, 128), F32),
            vmem((2, NI * UNIT, 128), F32),
            vmem((2, NP, 8, 256), F32),
            vmem((2, NP, 8, 256), F32),
            vmem((NP, NI // 2, 512, 256), BF16),
            vmem((SW, 2 * NI * UNIT), BF16),
            vmem((8, 8, 128), F32),
            vmem((16, 8, 128), F32),
            vmem((8, 8, 128), F32),
            vmem((16, 8, 128), F32),
            vmem((8, 8, 128), F32),
            vmem((16, 8, 128), F32),
            vmem((8, UNIT, SW), BF16),
            vmem((8, UNIT, SW), BF16),
            vmem((8, SW, UNIT), F32),
            vmem((8, SW, UNIT), F32),
            vmem((8, SW, UNIT), F32),
            vmem((8, SW, UNIT), BF16),
            vmem((8, SW, UNIT), BF16),
            vmem((2, 8, 128), F32),
            vmem((8, 8, 128), F32),
            vmem((16, 8, 128), F32),
            pltpu.SemaphoreType.DMA((4,)),
            pltpu.SemaphoreType.DMA((128,)),
            pltpu.SemaphoreType.DMA((128,)),
        ],
        compiler_params=pltpu.CompilerParams(
            collective_id=0, has_side_effects=True, vmem_limit_bytes=62 * 2**20
        ),
        cost_estimate=pl.CostEstimate(
            flops=16_000_000_000, bytes_accessed=1_500_000, transcendentals=20_000_000
        ),
    )(teacher_image, teacher_text, student_image, student_text)
    return loss[0, 0], image_grad, text_grad


def solution(mesh):
    in_specs = (
        P(("img", "txt"), None),
        P(("txt", "img"), None),
        P(("img", "txt"), None),
        P(("txt", "img"), None),
    )
    out_specs = (P(), P(("img", "txt"), None), P(("txt", "img"), None))
    return jax.shard_map(local, mesh=mesh, in_specs=in_specs, out_specs=out_specs, check_vma=False)
```

```python
import functools
import math

import jax
import jax.numpy as jnp
from jax import lax
from jax.experimental import pallas as pl
from jax.experimental.pallas import tpu as pltpu
from jax.sharding import PartitionSpec as P

MESH = pl.DeviceIdType.MESH
F32 = jnp.float32
BF16 = jnp.bfloat16
UNIT = 128
TW = 1280
SW = 512
W = TW + SW
NI = 8
NP = 8
LOG2E = 1.4426950408889634
LN2 = 0.6931471805599453
LOW = -1e30
CODE = 2.0**18
TINY = 1e-25


SLOTS = ((0, 0), (0, 1), (0, 3), (1, 0), (0, 2), (1, 1), (1, 3), (1, 2))
BACK = tuple(SLOTS.index((a, (4 - r) % 4)) for a, r in SLOTS)


def dot_nt(a, b):
    return lax.dot_general(a, b, (((1,), (1,)), ((), ())), preferred_element_type=F32)


def encode(v):
    v2 = v * v
    return (v2 * v2 * v).astype(BF16)


def decode(code):
    y = code.astype(F32)
    u = jnp.exp2(jnp.log2(jnp.abs(y)) * 0.2)
    return jnp.where(y < 0.0, -u, u)


def log_sum(peak, total):
    return peak + jnp.log2(total)


def kernel(
    pairs,
    ti, tt, si, st,
    out,
    img, txt, lt, ls, rm, rs, cm, cs, d, ist,
    rmsg, cmsg, rrx, crx, rlse, clse,
    isend, irecv, xsend, xrecv, keep, tsend, trecv,
    lsend, lrx_i, lrx_t, top,
    lsem, ssem, rsem,
):
    i_index, t_index = lax.axis_index("img"), lax.axis_index("txt")
    z, c, x, y = i_index // 2, i_index % 2, t_index // 4, t_index % 4
    xa = x + 1 - 2 * (x % 2)
    xb = 3 - x

    def i_peer(slot):
        a, r = SLOTS[slot]
        return (z * 2 + c, (xa if a else x) * 4 + (y + r) % 4)

    def t_peer(cc, slot):
        a, r = SLOTS[slot]
        return (((z + r) % 4) * 2 + (c + cc) % 2, (xb if a else x) * 4 + y)

    serial = [0]
    begun = []

    def send(src, dst, device):
        n = serial[0]
        serial[0] += 1
        copy = pltpu.make_async_remote_copy(
            src_ref=src, dst_ref=dst, send_sem=ssem.at[n], recv_sem=rsem.at[n],
            device_id=device, device_id_type=MESH,
        )
        copy.start()
        begun.append(copy)
        return copy

    def arrived(copies):
        for copy in copies:
            copy.wait_recv()

    loads = [
        pltpu.make_async_copy(ti, img.at[0, :, 0:TW], lsem.at[0]),
        pltpu.make_async_copy(si, img.at[0, :, TW:W], lsem.at[1]),
        pltpu.make_async_copy(tt, txt.at[0, :, 0:TW], lsem.at[2]),
        pltpu.make_async_copy(st, txt.at[0, :, TW:W], lsem.at[3]),
    ]
    for copy in loads:
        copy.start()
    barrier = pltpu.get_barrier_semaphore()
    neighbours = [i_peer(q) for q in (1, 2, 3)] + [t_peer(0, q) for q in (1, 2, 3)] + [t_peer(1, 0)]
    for device in neighbours:
        pl.semaphore_signal(barrier, inc=1, device_id=device, device_id_type=MESH)
    rm[...] = jnp.full(rm.shape, LOW, F32)
    rs[...] = jnp.zeros(rs.shape, F32)
    cm[...] = jnp.full(cm.shape, LOW, F32)
    cs[...] = jnp.zeros(cs.shape, F32)
    pl.semaphore_wait(barrier, 7)
    for copy in loads:
        copy.wait()

    def image_at(slot, rows=(0, 128), columns=(0, W)):
        return img.at[slot, rows[0] : rows[1], columns[0] : columns[1]]

    def text_at(slot, rows=(0, 128), columns=(0, W)):
        return txt.at[2 * slot, rows[0] : rows[1], columns[0] : columns[1]]

    low_rows, high_rows = (0, 64), (64, 128)
    teacher_part, student_part = (0, TW), (TW, W)
    sides = ((image_at, i_peer), (text_at, functools.partial(t_peer, 0)))
    crossings = []

    def cross(slot, columns=(0, W)):
        part = slice(columns[0], columns[1])
        crossings.append(
            send(txt.at[2 * slot, :, part], txt.at[2 * slot + 1, :, part], t_peer(1, 0))
        )

    flights = [{} for _ in sides]
    for first, second in ((low_rows, high_rows), (high_rows, low_rows)):
        for (at, peer), f in zip(sides, flights):
            f["minus", first] = send(at(0, first), at(1, first), peer(2))
            f["plus", second] = send(at(0, second), at(2, second), peer(1))
            f["side", first] = send(at(0, first), at(3, first), peer(3))
    cross(0)
    for (at, peer), f in zip(sides, flights):
        f["minus", low_rows].wait_recv()
        f["far", low_rows] = send(at(1, low_rows), at(4, low_rows), peer(2))
    for (at, peer), f in zip(sides, flights):
        f["plus", high_rows].wait_recv()
        f["far", high_rows] = send(at(2, high_rows), at(4, high_rows), peer(1))
    for (at, peer), f in zip(sides, flights):
        arrived([f["side", low_rows], f["side", high_rows]])
        for part in (teacher_part, student_part):
            f["side_minus", part] = send(
                at(3, columns=part), at(5, columns=part), peer(2)
            )
            f["side_plus", part] = send(
                at(3, columns=part), at(6, columns=part), peer(1)
            )
    for (at, peer), f in zip(sides, flights):
        arrived([f["minus", high_rows], f["plus", low_rows]])
    for slot in (3, 1, 2):
        cross(slot)

    scale_t = LOG2E * TW**-0.5
    scale_s = LOG2E * SW**-0.5

    def dots(model, p, u0, count):
        rows = slice(u0 * UNIT, (u0 + count) * UNIT)
        lanes = slice(TW, W) if model else slice(0, TW)
        width = SW if model else TW
        logit, scale = ((lt, scale_t), (ls, scale_s))[model]
        logit[p, rows, :] = scale * dot_nt(
            img[u0 : u0 + count, :, lanes].reshape(count * UNIT, width),
            txt[2 * p : 2 * p + 2, :, lanes].reshape(2 * UNIT, width),
        )

    def fold(model, p, u):
        logit = (lt, ls)[model]
        rows = slice(u * UNIT, (u + 1) * UNIT)
        left, right = logit[p, rows, 0:128], logit[p, rows, 128:256]
        old = rm[model, rows, :]
        new = jnp.maximum(old, jnp.maximum(left, right))
        rm[model, rows, :] = new
        rs[model, rows, :] = (
            rs[model, rows, :] * jnp.exp2(old - new) + jnp.exp2(left - new) + jnp.exp2(right - new)
        )
        for h, part in ((0, left), (1, right)):
            lanes = slice(h * 128, h * 128 + 128)
            part = part.reshape(16, 8, 128)
            old = cm[model, p, :, lanes]
            new = jnp.maximum(old, jnp.max(part, axis=0))
            cm[model, p, :, lanes] = new
            cs[model, p, :, lanes] = cs[model, p, :, lanes] * jnp.exp2(old - new) + jnp.sum(
                jnp.exp2(part - new[None]), axis=0
            )

    def blocks(todo):
        for model, p, u0, count in todo:
            dots(model, p, u0, count)
            for u in range(u0, u0 + count):
                fold(model, p, u)

    def largest(ref, count):
        best = jnp.zeros((8, SW), F32)
        for n in range(count):
            part = jnp.abs(ref[n, :, TW:W].astype(F32)).reshape(16, 8, SW)
            best = jnp.maximum(best, jnp.max(part, axis=0))
        return jnp.broadcast_to(jnp.max(best, axis=(0, 1), keepdims=True), (1, 128))

    arrived(crossings)
    crossings.clear()
    blocks([(model, p, 0, 4) for p in range(4) for model in range(2)])
    for (at, peer), f in zip(sides, flights):
        arrived([f["far", low_rows], f["far", high_rows]])
        for part in (teacher_part, student_part):
            f["side_far", part] = send(at(4, columns=part), at(7, columns=part), peer(3))
    cross(4)
    arrived(crossings)
    crossings.clear()
    blocks([(model, 4, 0, 5) for model in range(2)])
    blocks([(model, p, 4, 1) for p in range(4) for model in range(2)])

    for model, part in enumerate((teacher_part, student_part)):
        for (at, peer), f in reversed(list(zip(sides, flights))):
            for slot, name in ((5, "side_minus"), (6, "side_plus"), (7, "side_far")):
                f[name, part].wait_recv()
                if at is text_at:
                    cross(slot, part)
        blocks([(model, p, 5, 3) for p in range(5)])
        arrived(crossings)
        crossings.clear()
        blocks([(model, p, u0, 4) for p in range(5, 8) for u0 in (0, 4)])

    image_top = jnp.maximum(largest(img, NI), TINY)
    text_top = jnp.maximum(largest(txt, 2 * NP), TINY)
    top[0] = jnp.broadcast_to(image_top, (8, 128))
    top_flight = send(top.at[0], top.at[1], t_peer(1, 0))
    for slot, (a, r) in enumerate(SLOTS):
        rows = slice(slot * UNIT, slot * UNIT + UNIT)
        for model in range(2):
            peaks = rm[model, rows, :].T
            totals = rs[model, rows, :].T
            peak = jnp.max(peaks, axis=0, keepdims=True)
            total = jnp.sum(totals * jnp.exp2(peaks - peak), axis=0, keepdims=True)
            lse = log_sum(peak, total)
            for flip in range(2):
                row = (a ^ flip) * 2 + model
                rmsg[flip, r, row : row + 1, :] = lse
            peaks = cm[model, slot]
            peak = jnp.max(peaks, axis=0, keepdims=True)
            total = jnp.sum(cs[model, slot] * jnp.exp2(peaks - peak), axis=0, keepdims=True)
            lse = log_sum(peak, total)
            for cc in range(2):
                for flip in range(4):
                    row = (((cc * 2 + a) ^ flip) * 2) + model
                    cmsg[flip, r, row : row + 1, :] = lse[:, cc * 128 : cc * 128 + 128]
    for flip in range(2):
        for r in range(4):
            rmsg[flip, r, 4:8, :] = jnp.broadcast_to(text_top, (4, 128))

    flying = [
        send(cmsg.at[cc * 2 + SLOTS[q][0]], crx.at[2 * BACK[q] + cc], t_peer(cc, q))
        for q in range(7, -1, -1)
        for cc in range(2)
        if q or cc
    ]
    flying += [
        send(rmsg.at[SLOTS[q][0]], rrx.at[BACK[q]], i_peer(q)) for q in range(7, 0, -1)
    ]
    for b in range(NI // 2):
        turned = img[2 * b : 2 * b + 2, :, TW:W].reshape(2 * UNIT, SW).T
        ist[:, b * 512 : b * 512 + 256] = turned
        ist[:, b * 512 + 256 : b * 512 + 512] = turned
    arrived(flying)

    def combine(own, parts):
        peak = own
        for part in parts:
            peak = jnp.maximum(peak, part)
        total = jnp.exp2(own - peak)
        for part in parts:
            total = total + jnp.exp2(part - peak)
        return log_sum(peak, total)

    for r in range(4):
        rlse[r] = combine(
            rmsg[0, r], [rrx[q, (r - SLOTS[q][1]) % 4] for q in range(1, 8)]
        )
        clse[r] = combine(
            cmsg[0, r], [crx[j, (r - SLOTS[j // 2][1]) % 4] for j in range(1, 16)]
        )
    gap = (rlse[0, 1:2, :] - rlse[0, 0:1, :]) + (clse[0, 1:2, :] - clse[0, 0:1, :])

    image_code = CODE * SW**-0.5 / text_top[0:1, 0:1]
    grad_flights = []

    def tiles(b, p, rows_lse, diverge):
        rows = slice(b * 256, b * 256 + 256)
        a, r = SLOTS[p]
        lse_t, lse_s = rows_lse
        for h in range(2):
            lanes = slice(h * 128, h * 128 + 128)
            row = (h * 2 + a) * 2
            t = lt[p, rows, lanes]
            s = ls[p, rows, lanes]
            teacher = jnp.exp2(t - lse_t) + jnp.exp2(t - clse[r, row : row + 1, :])
            student = jnp.exp2(s - lse_s) + jnp.exp2(s - clse[r, row + 1 : row + 2, :])
            diverge = diverge + jnp.sum((teacher * (t - s)).reshape(32, 8, 128), axis=0)
            delta = student - teacher
            high = delta.astype(BF16)
            low = (delta - high.astype(F32)).astype(BF16)
            d[p, b, 0:256, lanes] = high
            d[p, b, 256:512, lanes] = low
        return diverge

    def turned_lse(b):
        found = []
        for model in range(2):
            columns = []
            for slot in (2 * b, 2 * b + 1):
                a, r = SLOTS[slot]
                row = 2 * a + model
                columns.append(jnp.broadcast_to(rlse[r, row : row + 1, :], (128, 128)).T)
            found.append(jnp.concatenate(columns, axis=0))
        return found

    diverge = jnp.zeros((8, 128), F32)
    rows_lse = turned_lse(3)
    for p in range(NP):
        diverge = tiles(3, p, rows_lse, diverge)
    for b in (3, 2, 1, 0):
        total = jnp.zeros((512, SW), F32)
        rows_lse = turned_lse(b - 1) if b else None
        for p in range(NP):
            if b:
                diverge = tiles(b - 1, p, rows_lse, diverge)
            weights = txt[2 * p : 2 * p + 2, :, TW:W].reshape(2 * UNIT, SW)
            total = total + jnp.dot(d[p, b], weights, preferred_element_type=F32)
        total = total[0:256] + total[256:512]
        for h in (1, 0):
            slot = 2 * b + h
            part = total[h * 128 : h * 128 + 128]
            if slot == 0:
                out[0:UNIT] = part
            else:
                isend[slot] = encode(part * image_code)
                grad_flights.append(send(isend.at[slot], irecv.at[BACK[slot]], i_peer(slot)))

    first_row = lax.broadcasted_iota(jnp.int32, (8, 128), 0) == 0
    lsend[0, 0:8] = diverge + jnp.where(first_row, jnp.broadcast_to(gap, (8, 128)), 0.0)
    loss_flights = [
        send(lsend.at[0, 0:8], lrx_i.at[BACK[q]], i_peer(q)) for q in range(7, 0, -1)
    ]
    top_flight.wait_recv()
    chip_top = jnp.maximum(image_top, top[1, 0:1, :])
    text_code = CODE * SW**-0.5 / chip_top[0:1, 0:1]

    crossed = {}

    def pass_on(slot):
        crossed[slot].wait_recv()
        part = keep[slot] + xrecv[slot]
        if slot == 0:
            keep[0] = part
        else:
            tsend[slot] = encode(part * text_code)
            grad_flights.append(send(tsend.at[slot], trecv.at[BACK[slot]], t_peer(0, slot)))

    for p in range(NP - 1, -1, -1):
        part = jnp.dot(ist[...], d[p].reshape(2048, 256), preferred_element_type=F32)
        keep[p] = part[:, 0:128]
        xsend[p] = part[:, 128:256]
        crossed[p] = send(xsend.at[p], xrecv.at[p], t_peer(1, 0))
        if p < NP - 1:
            pass_on(p + 1)
        if p == 3:
            arrived(loss_flights)
            loss_part = lsend[0, 0:8]
            for q in range(1, 8):
                loss_part = loss_part + lrx_i[q]
            lsend[1, 0:8] = loss_part
            lsend[1, 8:16] = jnp.broadcast_to(chip_top, (8, 128))
            loss_flights = [
                send(lsend.at[1], lrx_t.at[2 * BACK[j // 2] + j % 2], t_peer(j % 2, j // 2))
                for j in range(15, 0, -1)
            ]
    pass_on(0)

    arrived(loss_flights)
    loss_part = lsend[1, 0:8]
    for q in range(1, 16):
        loss_part = loss_part + lrx_t[q, 0:8]
    loss = jnp.sum(loss_part, axis=(0, 1), keepdims=True) * (LN2 / (2.0 * pairs))
    out[2 * UNIT : 2 * UNIT + 8] = jnp.broadcast_to(loss, (8, SW))

    arrived(grad_flights)
    image_total = out[0:UNIT] * SW**-0.5
    text_total = keep[0] * SW**-0.5
    for q in range(1, 8):
        image_total = image_total + decode(irecv[q]) * (rrx[q, 0, 4:5, 0:1] * (1.0 / CODE))
        text_total = text_total + decode(trecv[q]) * (lrx_t[2 * q, 8:9, 0:1] * (1.0 / CODE))
    out[0:UNIT] = image_total
    out[UNIT : 2 * UNIT] = text_total.T
    for copy in begun:
        copy.wait_send()


def local(teacher_image, teacher_text, student_image, student_text):
    pairs = teacher_image.shape[0] * lax.axis_size("img") * lax.axis_size("txt")
    vmem = pltpu.VMEM
    result = pl.pallas_call(
        functools.partial(kernel, pairs),
        out_shape=jax.ShapeDtypeStruct((2 * UNIT + 8, SW), F32),
        in_specs=[pl.BlockSpec(memory_space=pl.ANY)] * 4,
        out_specs=pl.BlockSpec(memory_space=vmem),
        scratch_shapes=[
            vmem((NI, UNIT, W), BF16),
            vmem((2 * NP, UNIT, W), BF16),
            vmem((NP, NI * UNIT, 256), F32),
            vmem((NP, NI * UNIT, 256), F32),
            vmem((2, NI * UNIT, 128), F32),
            vmem((2, NI * UNIT, 128), F32),
            vmem((2, NP, 8, 256), F32),
            vmem((2, NP, 8, 256), F32),
            vmem((NP, NI // 2, 512, 256), BF16),
            vmem((SW, 2 * NI * UNIT), BF16),
            vmem((2, 4, 8, 128), F32),
            vmem((4, 4, 8, 128), F32),
            vmem((8, 4, 8, 128), F32),
            vmem((16, 4, 8, 128), F32),
            vmem((4, 8, 128), F32),
            vmem((4, 8, 128), F32),
            vmem((8, UNIT, SW), BF16),
            vmem((8, UNIT, SW), BF16),
            vmem((8, SW, UNIT), F32),
            vmem((8, SW, UNIT), F32),
            vmem((8, SW, UNIT), F32),
            vmem((8, SW, UNIT), BF16),
            vmem((8, SW, UNIT), BF16),
            vmem((2, 16, 128), F32),
            vmem((8, 8, 128), F32),
            vmem((16, 16, 128), F32),
            vmem((2, 8, 128), F32),
            pltpu.SemaphoreType.DMA((4,)),
            pltpu.SemaphoreType.DMA((128,)),
            pltpu.SemaphoreType.DMA((128,)),
        ],
        compiler_params=pltpu.CompilerParams(
            collective_id=0, has_side_effects=True, vmem_limit_bytes=62 * 2**20
        ),
        cost_estimate=pl.CostEstimate(
            flops=16_000_000_000, bytes_accessed=1_500_000, transcendentals=20_000_000
        ),
    )(teacher_image, teacher_text, student_image, student_text)
    return result[2 * UNIT, 0], result[0:UNIT], result[UNIT : 2 * UNIT]


def solution(mesh):
    in_specs = (
        P(("img", "txt"), None),
        P(("txt", "img"), None),
        P(("img", "txt"), None),
        P(("txt", "img"), None),
    )
    out_specs = (P(), P(("img", "txt"), None), P(("txt", "img"), None))
    return jax.shard_map(local, mesh=mesh, in_specs=in_specs, out_specs=out_specs, check_vma=False)
```

```python
import functools
import math

import jax
import jax.numpy as jnp
from jax import lax
from jax.experimental import pallas as pl
from jax.experimental.pallas import tpu as pltpu
from jax.sharding import PartitionSpec as P

MESH = pl.DeviceIdType.MESH
F32 = jnp.float32
BF16 = jnp.bfloat16
UNIT = 128
TW = 1280
SW = 512
W = TW + SW
NI = 8
NP = 8
LOG2E = 1.4426950408889634
LN2 = 0.6931471805599453
LOW = -1e30
CODE = 2.0**18
TINY = 1e-25


SLOTS = ((0, 0), (0, 1), (0, 3), (1, 0), (0, 2), (1, 1), (1, 3), (1, 2))
BACK = tuple(SLOTS.index((a, (4 - r) % 4)) for a, r in SLOTS)


def dot_nt(a, b):
    return lax.dot_general(a, b, (((1,), (1,)), ((), ())), preferred_element_type=F32)


def encode(v):
    v2 = v * v
    return (v2 * v2 * v).astype(BF16)


def decode(code):
    y = code.astype(F32)
    u = jnp.exp2(jnp.log2(jnp.abs(y)) * 0.2)
    return jnp.where(y < 0.0, -u, u)


def log_sum(peak, total):
    return peak + jnp.log2(total)


def kernel(
    pairs,
    ti, tt, si, st,
    out,
    img, txt, lt, ls, rm, rs, cm, cs, d, ist,
    rmsg, cmsg, rrx, crx, rlse, clse,
    isend, irecv, xsend, xrecv, keep, tsend, trecv,
    lsend, lrx_i, lrx_t, top,
    lsem, ssem, rsem,
):
    i_index, t_index = lax.axis_index("img"), lax.axis_index("txt")
    z, c, x, y = i_index // 2, i_index % 2, t_index // 4, t_index % 4
    xa = x + 1 - 2 * (x % 2)
    xb = 3 - x

    def i_peer(slot):
        a, r = SLOTS[slot]
        return (z * 2 + c, (xa if a else x) * 4 + (y + r) % 4)

    def t_peer(cc, slot):
        a, r = SLOTS[slot]
        return (((z + r) % 4) * 2 + (c + cc) % 2, (xb if a else x) * 4 + y)

    serial = [0]
    begun = []

    def send(src, dst, device):
        n = serial[0]
        serial[0] += 1
        copy = pltpu.make_async_remote_copy(
            src_ref=src, dst_ref=dst, send_sem=ssem.at[n], recv_sem=rsem.at[n],
            device_id=device, device_id_type=MESH,
        )
        copy.start()
        begun.append(copy)
        return copy

    def arrived(copies):
        for copy in copies:
            copy.wait_recv()

    loads = [
        pltpu.make_async_copy(ti, img.at[0, :, 0:TW], lsem.at[0]),
        pltpu.make_async_copy(si, img.at[0, :, TW:W], lsem.at[1]),
        pltpu.make_async_copy(tt, txt.at[0, :, 0:TW], lsem.at[2]),
        pltpu.make_async_copy(st, txt.at[0, :, TW:W], lsem.at[3]),
    ]
    for copy in loads:
        copy.start()
    barrier = pltpu.get_barrier_semaphore()
    neighbours = [i_peer(q) for q in (1, 2, 3)] + [t_peer(0, q) for q in (1, 2, 3)] + [t_peer(1, 0)]
    for device in neighbours:
        pl.semaphore_signal(barrier, inc=1, device_id=device, device_id_type=MESH)
    rm[...] = jnp.full(rm.shape, LOW, F32)
    rs[...] = jnp.zeros(rs.shape, F32)
    cm[...] = jnp.full(cm.shape, LOW, F32)
    cs[...] = jnp.zeros(cs.shape, F32)
    rmsg[...] = jnp.zeros(rmsg.shape, F32)
    pl.semaphore_wait(barrier, 7)
    for copy in loads:
        copy.wait()

    def image_at(slot, rows=(0, 128), columns=(0, W)):
        return img.at[slot, rows[0] : rows[1], columns[0] : columns[1]]

    def text_at(slot, rows=(0, 128), columns=(0, W)):
        return txt.at[2 * slot, rows[0] : rows[1], columns[0] : columns[1]]

    low_rows, high_rows = (0, 64), (64, 128)
    third_rows, last_rows, second_rows, first_rows = (64, 96), (96, 128), (32, 64), (0, 32)
    minus_relief, plus_relief = (0, 16), (112, 128)
    minus_rest, plus_rest = (16, 128), (0, 112)
    teacher_part, student_part = (0, TW), (TW, W)
    sides = ((image_at, i_peer), (text_at, functools.partial(t_peer, 0)))
    crossings = []

    def cross(slot, columns=(0, W)):
        part = slice(columns[0], columns[1])
        crossings.append(
            send(txt.at[2 * slot, :, part], txt.at[2 * slot + 1, :, part], t_peer(1, 0))
        )

    flights = [{} for _ in sides]
    for (at, peer), f in zip(sides, flights):
        f["minus", 0] = send(at(0, low_rows), at(1, low_rows), peer(2))
        f["plus", 0] = send(at(0, high_rows), at(2, high_rows), peer(1))
        f["side", 0] = send(at(0, low_rows), at(3, low_rows), peer(3))
    for (at, peer), f in zip(sides, flights):
        f["minus", 1] = send(at(0, third_rows), at(1, third_rows), peer(2))
        f["plus", 1] = send(at(0, second_rows), at(2, second_rows), peer(1))
        f["side", 1] = send(at(0, high_rows), at(3, high_rows), peer(3))
    cross(0)
    for (at, peer), f in zip(sides, flights):
        f["minus", 0].wait_recv()
        f["far", 0] = send(at(1, low_rows), at(4, low_rows), peer(2))
        f["relief", 0] = send(at(1, minus_relief), at(5, minus_relief), peer(3))
        f["minus", 2] = send(at(0, last_rows), at(1, last_rows), peer(2))
    for (at, peer), f in zip(sides, flights):
        f["plus", 0].wait_recv()
        f["far", 1] = send(at(2, high_rows), at(4, high_rows), peer(1))
        f["relief", 1] = send(at(2, plus_relief), at(6, plus_relief), peer(3))
        f["plus", 2] = send(at(0, first_rows), at(2, first_rows), peer(1))
    for (at, peer), f in zip(sides, flights):
        arrived([f["side", 0], f["side", 1]])
        for part in (teacher_part, student_part):
            f["side_minus", part] = send(at(3, minus_rest, part), at(5, minus_rest, part), peer(2))
            f["side_plus", part] = send(at(3, plus_rest, part), at(6, plus_rest, part), peer(1))
    cross(3)
    for (at, peer), f in zip(sides, flights):
        for n, rows in enumerate((low_rows, high_rows)):
            f["far", n].wait_recv()
            f["side_far", n, teacher_part] = send(
                at(4, rows, teacher_part), at(7, rows, teacher_part), peer(3)
            )
    for (at, peer), f in zip(sides, flights):
        for n, rows in enumerate((low_rows, high_rows)):
            f["side_far", n, student_part] = send(
                at(4, rows, student_part), at(7, rows, student_part), peer(3)
            )
    cross(4)
    for (at, peer), f in reversed(list(zip(sides, flights))):
        arrived([f["minus", 1], f["plus", 1], f["minus", 2], f["plus", 2]])
        if at is text_at:
            cross(1)
            cross(2)

    scale_t = LOG2E * TW**-0.5
    scale_s = LOG2E * SW**-0.5

    def dots(model, p, u0, count):
        rows = slice(u0 * UNIT, (u0 + count) * UNIT)
        lanes = slice(TW, W) if model else slice(0, TW)
        width = SW if model else TW
        logit, scale = ((lt, scale_t), (ls, scale_s))[model]
        logit[p, rows, :] = scale * dot_nt(
            img[u0 : u0 + count, :, lanes].reshape(count * UNIT, width),
            txt[2 * p : 2 * p + 2, :, lanes].reshape(2 * UNIT, width),
        )

    def fold(model, p, u):
        logit = (lt, ls)[model]
        rows = slice(u * UNIT, (u + 1) * UNIT)
        left, right = logit[p, rows, 0:128], logit[p, rows, 128:256]
        old = rm[model, rows, :]
        new = jnp.maximum(old, jnp.maximum(left, right))
        rm[model, rows, :] = new
        rs[model, rows, :] = (
            rs[model, rows, :] * jnp.exp2(old - new) + jnp.exp2(left - new) + jnp.exp2(right - new)
        )
        for h, part in ((0, left), (1, right)):
            lanes = slice(h * 128, h * 128 + 128)
            part = part.reshape(16, 8, 128)
            old = cm[model, p, :, lanes]
            new = jnp.maximum(old, jnp.max(part, axis=0))
            cm[model, p, :, lanes] = new
            cs[model, p, :, lanes] = cs[model, p, :, lanes] * jnp.exp2(old - new) + jnp.sum(
                jnp.exp2(part - new[None]), axis=0
            )

    def blocks(todo):
        for model, p, u0, count in todo:
            dots(model, p, u0, count)
            for u in range(u0, u0 + count):
                fold(model, p, u)

    def largest(ref, count):
        best = jnp.zeros((8, SW), F32)
        for n in range(count):
            part = jnp.abs(ref[n, :, TW:W].astype(F32)).reshape(16, 8, SW)
            best = jnp.maximum(best, jnp.max(part, axis=0))
        return jnp.broadcast_to(jnp.max(best, axis=(0, 1), keepdims=True), (1, 128))

    arrived(crossings)
    crossings.clear()
    blocks([(model, p, 0, 5) for p in range(5) for model in range(2)])

    for model, part in enumerate((teacher_part, student_part)):
        for (at, peer), f in reversed(list(zip(sides, flights))):
            for slot, names in (
                (5, (("relief", 0), ("side_minus", part))),
                (6, (("relief", 1), ("side_plus", part))),
                (7, (("side_far", 0, part), ("side_far", 1, part))),
            ):
                arrived([f[name] for name in names if model == 0 or name[0] != "relief"])
                if at is text_at:
                    cross(slot, part)
        blocks([(model, p, 5, 3) for p in range(5)])
        arrived(crossings)
        crossings.clear()
        blocks([(model, p, u0, 4) for p in range(5, 8) for u0 in (0, 4)])

    for slot, (a, r) in enumerate(SLOTS):
        rows = slice(slot * UNIT, slot * UNIT + UNIT)
        for model in range(2):
            peaks = rm[model, rows, :].T
            totals = rs[model, rows, :].T
            peak = jnp.max(peaks, axis=0, keepdims=True)
            total = jnp.sum(totals * jnp.exp2(peaks - peak), axis=0, keepdims=True)
            lse = log_sum(peak, total)
            for flip in range(2):
                row = (a ^ flip) * 2 + model
                rmsg[flip, r, row : row + 1, :] = lse
            peaks = cm[model, slot]
            peak = jnp.max(peaks, axis=0, keepdims=True)
            total = jnp.sum(cs[model, slot] * jnp.exp2(peaks - peak), axis=0, keepdims=True)
            lse = log_sum(peak, total)
            for cc in range(2):
                for flip in range(4):
                    row = (((cc * 2 + a) ^ flip) * 2) + model
                    cmsg[flip, r, row : row + 1, :] = lse[:, cc * 128 : cc * 128 + 128]

    flying = [
        send(cmsg.at[cc * 2 + SLOTS[q][0]], crx.at[2 * BACK[q] + cc], t_peer(cc, q))
        for q in range(7, -1, -1)
        for cc in range(2)
        if q or cc
    ]
    flying += [
        send(rmsg.at[SLOTS[q][0]], rrx.at[BACK[q]], i_peer(q)) for q in range(7, 0, -1)
    ]
    image_top = jnp.maximum(largest(img, NI), TINY)
    text_top = jnp.maximum(largest(txt, 2 * NP), TINY)
    top[0] = jnp.broadcast_to(image_top, (8, 128))
    top_flight = send(top.at[0], top.at[1], t_peer(1, 0))
    for b in range(NI // 2):
        turned = img[2 * b : 2 * b + 2, :, TW:W].reshape(2 * UNIT, SW).T
        ist[:, b * 512 : b * 512 + 256] = turned
        ist[:, b * 512 + 256 : b * 512 + 512] = turned
    arrived(flying)

    def combine(own, parts):
        peak = own
        for part in parts:
            peak = jnp.maximum(peak, part)
        total = jnp.exp2(own - peak)
        for part in parts:
            total = total + jnp.exp2(part - peak)
        return log_sum(peak, total)

    for r in range(4):
        rlse[r] = combine(
            rmsg[0, r], [rrx[q, (r - SLOTS[q][1]) % 4] for q in range(1, 8)]
        )
        clse[r] = combine(
            cmsg[0, r], [crx[j, (r - SLOTS[j // 2][1]) % 4] for j in range(1, 16)]
        )
    gap = (rlse[0, 1:2, :] - rlse[0, 0:1, :]) + (clse[0, 1:2, :] - clse[0, 0:1, :])

    image_code = CODE * SW**-0.5 / text_top[0:1, 0:1]
    image_flights, text_flights = [], []

    def tiles(b, p, rows_lse, diverge):
        rows = slice(b * 256, b * 256 + 256)
        a, r = SLOTS[p]
        lse_t, lse_s = rows_lse
        for h in range(2):
            lanes = slice(h * 128, h * 128 + 128)
            row = (h * 2 + a) * 2
            t = lt[p, rows, lanes]
            s = ls[p, rows, lanes]
            teacher = jnp.exp2(t - lse_t) + jnp.exp2(t - clse[r, row : row + 1, :])
            student = jnp.exp2(s - lse_s) + jnp.exp2(s - clse[r, row + 1 : row + 2, :])
            diverge = diverge + jnp.sum((teacher * (t - s)).reshape(32, 8, 128), axis=0)
            delta = student - teacher
            high = delta.astype(BF16)
            low = (delta - high.astype(F32)).astype(BF16)
            d[p, b, 0:256, lanes] = high
            d[p, b, 256:512, lanes] = low
        return diverge

    def turned_lse(b):
        found = []
        for model in range(2):
            columns = []
            for slot in (2 * b, 2 * b + 1):
                a, r = SLOTS[slot]
                row = 2 * a + model
                columns.append(jnp.broadcast_to(rlse[r, row : row + 1, :], (128, 128)).T)
            found.append(jnp.concatenate(columns, axis=0))
        return found

    FAR, NEAR = (7, 6, 5, 4), (3, 2, 1, 0)
    row_lse = {}

    def delta_tiles(b, pairs_of_text, diverge):
        if b not in row_lse:
            row_lse[b] = turned_lse(b)
        for p in pairs_of_text:
            diverge = tiles(b, p, row_lse[b], diverge)
        return diverge

    def image_dot(total, b, p):
        weights = txt[2 * p : 2 * p + 2, :, TW:W].reshape(2 * UNIT, SW)
        return total + jnp.dot(d[p, b], weights, preferred_element_type=F32)

    def image_send(total, b):
        total = total[0:256] + total[256:512]
        for h in (1, 0):
            slot = 2 * b + h
            part = total[h * 128 : h * 128 + 128]
            if slot == 0:
                out[0:UNIT] = part
            else:
                isend[slot] = encode(part * image_code)
                image_flights.append(send(isend.at[slot], irecv.at[BACK[slot]], i_peer(slot)))

    crossed = {}

    def text_part(p):
        part = jnp.dot(ist[...], d[p].reshape(2048, 256), preferred_element_type=F32)
        keep[p] = part[:, 0:128]
        xsend[p] = part[:, 128:256]

    def text_cross(p):
        crossed[p] = send(xsend.at[p], xrecv.at[p], t_peer(1, 0))

    def text_send(slot):
        crossed[slot].wait_recv()
        part = keep[slot] + xrecv[slot]
        if slot == 0:
            keep[0] = part
        else:
            tsend[slot] = encode(part * text_code)
            text_flights.append(send(tsend.at[slot], trecv.at[BACK[slot]], t_peer(0, slot)))

    diverge = jnp.zeros((8, 128), F32)
    diverge = delta_tiles(3, FAR + NEAR, diverge)
    total = jnp.zeros((512, SW), F32)
    for n, p in enumerate(FAR + NEAR):
        diverge = delta_tiles(2, (p,), diverge)
        total = image_dot(total, 3, p)
    image_send(total, 3)
    total = jnp.zeros((512, SW), F32)
    for n, p in enumerate(FAR + NEAR):
        if n < 4:
            diverge = delta_tiles(1, (p,), diverge)
            diverge = delta_tiles(0, (p,), diverge)
        total = image_dot(total, 2, p)
    image_send(total, 2)
    top_flight.wait_recv()
    chip_top = jnp.maximum(image_top, top[1, 0:1, :])
    text_code = CODE * SW**-0.5 / chip_top[0:1, 0:1]
    for some, others in ((FAR[:2], NEAR[:2]), (FAR[2:], NEAR[2:])):
        for p in others:
            diverge = delta_tiles(1, (p,), diverge)
            diverge = delta_tiles(0, (p,), diverge)
        for p in some:
            text_part(p)
        for p in some:
            text_cross(p)
    text_send(7)
    text_send(6)
    first_row = lax.broadcasted_iota(jnp.int32, (8, 128), 0) == 0
    lsend[0, 0:8] = diverge + jnp.where(first_row, jnp.broadcast_to(gap, (8, 128)), 0.0)
    lsend[0, 8:16] = jnp.broadcast_to(text_top, (8, 128))
    loss_flights = [send(lsend.at[0], lrx_i.at[BACK[q]], i_peer(q)) for q in range(7, 0, -1)]
    total = jnp.zeros((512, SW), F32)
    for p in FAR + NEAR:
        total = image_dot(total, 1, p)
    image_send(total, 1)
    text_send(5)
    text_send(4)
    total = jnp.zeros((512, SW), F32)
    for p in FAR + NEAR:
        total = image_dot(total, 0, p)
    text_part(3)
    text_part(2)
    image_send(total, 0)
    text_cross(3)
    text_cross(2)
    text_part(1)
    text_part(0)
    text_cross(1)
    text_cross(0)
    for slot in NEAR:
        text_send(slot)

    arrived(loss_flights)
    loss_part = lsend[0, 0:8]
    for q in range(1, 8):
        loss_part = loss_part + lrx_i[q, 0:8]
    lsend[1, 0:8] = loss_part
    lsend[1, 8:16] = jnp.broadcast_to(chip_top, (8, 128))
    loss_flights = [
        send(lsend.at[1], lrx_t.at[2 * BACK[j // 2] + j % 2], t_peer(j % 2, j // 2))
        for j in range(15, 0, -1)
    ]

    image_total = out[0:UNIT] * SW**-0.5
    for q, flight in zip([BACK[q] for q in (7, 6, 5, 4, 3, 2, 1)], image_flights):
        flight.wait_recv()
        image_total = image_total + decode(irecv[q]) * (lrx_i[q, 8:9, 0:1] * (1.0 / CODE))
    out[0:UNIT] = image_total
    arrived(loss_flights)
    loss_part = lsend[1, 0:8]
    for q in range(1, 16):
        loss_part = loss_part + lrx_t[q, 0:8]
    loss = jnp.sum(loss_part, axis=(0, 1), keepdims=True) * (LN2 / (2.0 * pairs))
    out[2 * UNIT : 2 * UNIT + 8] = jnp.broadcast_to(loss, (8, SW))
    text_total = keep[0] * SW**-0.5
    for q, flight in zip([BACK[q] for q in (7, 6, 5, 4, 3, 2, 1)], text_flights):
        flight.wait_recv()
        text_total = text_total + decode(trecv[q]) * (lrx_t[2 * q, 8:9, 0:1] * (1.0 / CODE))
    out[UNIT : 2 * UNIT] = text_total.T
    for copy in begun:
        copy.wait_send()


def local(teacher_image, teacher_text, student_image, student_text):
    pairs = teacher_image.shape[0] * lax.axis_size("img") * lax.axis_size("txt")
    vmem = pltpu.VMEM
    result = pl.pallas_call(
        functools.partial(kernel, pairs),
        out_shape=jax.ShapeDtypeStruct((2 * UNIT + 8, SW), F32),
        in_specs=[pl.BlockSpec(memory_space=pl.ANY)] * 4,
        out_specs=pl.BlockSpec(memory_space=vmem),
        scratch_shapes=[
            vmem((NI, UNIT, W), BF16),
            vmem((2 * NP, UNIT, W), BF16),
            vmem((NP, NI * UNIT, 256), F32),
            vmem((NP, NI * UNIT, 256), F32),
            vmem((2, NI * UNIT, 128), F32),
            vmem((2, NI * UNIT, 128), F32),
            vmem((2, NP, 8, 256), F32),
            vmem((2, NP, 8, 256), F32),
            vmem((NP, NI // 2, 512, 256), BF16),
            vmem((SW, 2 * NI * UNIT), BF16),
            vmem((2, 4, 8, 128), F32),
            vmem((4, 4, 8, 128), F32),
            vmem((8, 4, 8, 128), F32),
            vmem((16, 4, 8, 128), F32),
            vmem((4, 8, 128), F32),
            vmem((4, 8, 128), F32),
            vmem((8, UNIT, SW), BF16),
            vmem((8, UNIT, SW), BF16),
            vmem((8, SW, UNIT), F32),
            vmem((8, SW, UNIT), F32),
            vmem((8, SW, UNIT), F32),
            vmem((8, SW, UNIT), BF16),
            vmem((8, SW, UNIT), BF16),
            vmem((2, 16, 128), F32),
            vmem((8, 16, 128), F32),
            vmem((16, 16, 128), F32),
            vmem((2, 8, 128), F32),
            pltpu.SemaphoreType.DMA((4,)),
            pltpu.SemaphoreType.DMA((128,)),
            pltpu.SemaphoreType.DMA((128,)),
        ],
        compiler_params=pltpu.CompilerParams(
            collective_id=0, has_side_effects=True, vmem_limit_bytes=62 * 2**20
        ),
        cost_estimate=pl.CostEstimate(
            flops=16_000_000_000, bytes_accessed=1_500_000, transcendentals=20_000_000
        ),
    )(teacher_image, teacher_text, student_image, student_text)
    return result[2 * UNIT, 0], result[0:UNIT], result[UNIT : 2 * UNIT]


def solution(mesh):
    in_specs = (
        P(("img", "txt"), None),
        P(("txt", "img"), None),
        P(("img", "txt"), None),
        P(("txt", "img"), None),
    )
    out_specs = (P(), P(("img", "txt"), None), P(("txt", "img"), None))
    return jax.shard_map(local, mesh=mesh, in_specs=in_specs, out_specs=out_specs, check_vma=False)
```

```python
import functools
import math

import jax
import jax.numpy as jnp
from jax import lax
from jax.experimental import pallas as pl
from jax.experimental.pallas import tpu as pltpu
from jax.sharding import PartitionSpec as P

MESH = pl.DeviceIdType.MESH
F32 = jnp.float32
BF16 = jnp.bfloat16
UNIT = 128
TW = 1280
SW = 512
W = TW + SW
NI = 8
NP = 8
LOG2E = 1.4426950408889634
LN2 = 0.6931471805599453
LOW = -1e30
CODE = 2.0**18
TINY = 1e-25


SLOTS = ((0, 0), (0, 1), (0, 3), (1, 0), (0, 2), (1, 1), (1, 3), (1, 2))
BACK = tuple(SLOTS.index((a, (4 - r) % 4)) for a, r in SLOTS)


def dot_nt(a, b):
    return lax.dot_general(a, b, (((1,), (1,)), ((), ())), preferred_element_type=F32)


def encode(v):
    v2 = v * v
    return (v2 * v2 * v).astype(BF16)


def decode(code):
    y = code.astype(F32)
    u = jnp.exp2(jnp.log2(jnp.abs(y)) * 0.2)
    return jnp.where(y < 0.0, -u, u)


def log_sum(peak, total):
    return peak + jnp.log2(total)


def kernel(
    pairs,
    ti, tt, si, st,
    out,
    img, txt, lt, ls, rm, rs, cm, cs, d, ist,
    rmsg, cmsg, rrx, crx, rlse, clse,
    isend, irecv, xsend, xrecv, keep, tsend, trecv,
    lsend, lrx_i, lrx_t, top,
    lsem, ssem, rsem,
):
    i_index, t_index = lax.axis_index("img"), lax.axis_index("txt")
    z, c, x, y = i_index // 2, i_index % 2, t_index // 4, t_index % 4
    xa = x + 1 - 2 * (x % 2)
    xb = 3 - x

    def i_peer(slot):
        a, r = SLOTS[slot]
        return (z * 2 + c, (xa if a else x) * 4 + (y + r) % 4)

    def t_peer(cc, slot):
        a, r = SLOTS[slot]
        return (((z + r) % 4) * 2 + (c + cc) % 2, (xb if a else x) * 4 + y)

    serial = [0]
    begun = []

    def send(src, dst, device):
        n = serial[0]
        serial[0] += 1
        copy = pltpu.make_async_remote_copy(
            src_ref=src, dst_ref=dst, send_sem=ssem.at[n], recv_sem=rsem.at[n],
            device_id=device, device_id_type=MESH,
        )
        copy.start()
        begun.append(copy)
        return copy

    def arrived(copies):
        for copy in copies:
            copy.wait_recv()

    loads = [
        pltpu.make_async_copy(ti, img.at[0, :, 0:TW], lsem.at[0]),
        pltpu.make_async_copy(si, img.at[0, :, TW:W], lsem.at[1]),
        pltpu.make_async_copy(tt, txt.at[0, :, 0:TW], lsem.at[2]),
        pltpu.make_async_copy(st, txt.at[0, :, TW:W], lsem.at[3]),
    ]
    for copy in loads:
        copy.start()
    barrier = pltpu.get_barrier_semaphore()
    neighbours = [i_peer(q) for q in (1, 2, 3)] + [t_peer(0, q) for q in (1, 2, 3)] + [t_peer(1, 0)]
    for device in neighbours:
        pl.semaphore_signal(barrier, inc=1, device_id=device, device_id_type=MESH)
    rm[...] = jnp.full(rm.shape, LOW, F32)
    rs[...] = jnp.zeros(rs.shape, F32)
    cm[...] = jnp.full(cm.shape, LOW, F32)
    cs[...] = jnp.zeros(cs.shape, F32)
    rmsg[...] = jnp.zeros(rmsg.shape, F32)
    pl.semaphore_wait(barrier, 7)
    for copy in loads:
        copy.wait()

    def image_at(slot, rows=(0, 128), columns=(0, W)):
        return img.at[slot, rows[0] : rows[1], columns[0] : columns[1]]

    def text_at(slot, rows=(0, 128), columns=(0, W)):
        return txt.at[2 * slot, rows[0] : rows[1], columns[0] : columns[1]]

    low_rows, high_rows = (0, 64), (64, 128)
    third_rows, last_rows, second_rows, first_rows = (64, 96), (96, 128), (32, 64), (0, 32)
    minus_relief, plus_relief = (0, 16), (112, 128)
    minus_rest, plus_rest = (16, 128), (0, 112)
    teacher_part, student_part = (0, TW), (TW, W)
    sides = ((image_at, i_peer), (text_at, functools.partial(t_peer, 0)))
    crossings = []

    def cross(slot, columns=(0, W)):
        part = slice(columns[0], columns[1])
        crossings.append(
            send(txt.at[2 * slot, :, part], txt.at[2 * slot + 1, :, part], t_peer(1, 0))
        )

    flights = [{} for _ in sides]
    for (at, peer), f in zip(sides, flights):
        f["minus", 0] = send(at(0, low_rows), at(1, low_rows), peer(2))
        f["plus", 0] = send(at(0, high_rows), at(2, high_rows), peer(1))
        f["side", 0] = send(at(0, low_rows), at(3, low_rows), peer(3))
    for (at, peer), f in zip(sides, flights):
        f["minus", 1] = send(at(0, third_rows), at(1, third_rows), peer(2))
        f["plus", 1] = send(at(0, second_rows), at(2, second_rows), peer(1))
        f["side", 1] = send(at(0, high_rows), at(3, high_rows), peer(3))
    cross(0)
    for (at, peer), f in zip(sides, flights):
        f["minus", 0].wait_recv()
        f["far", 0] = send(at(1, low_rows), at(4, low_rows), peer(2))
        f["relief", 0] = send(at(1, minus_relief), at(5, minus_relief), peer(3))
        f["minus", 2] = send(at(0, last_rows), at(1, last_rows), peer(2))
    for (at, peer), f in zip(sides, flights):
        f["plus", 0].wait_recv()
        f["far", 1] = send(at(2, high_rows), at(4, high_rows), peer(1))
        f["relief", 1] = send(at(2, plus_relief), at(6, plus_relief), peer(3))
        f["plus", 2] = send(at(0, first_rows), at(2, first_rows), peer(1))
    for (at, peer), f in zip(sides, flights):
        arrived([f["side", 0], f["side", 1]])
        for part in (teacher_part, student_part):
            f["side_minus", part] = send(at(3, minus_rest, part), at(5, minus_rest, part), peer(2))
            f["side_plus", part] = send(at(3, plus_rest, part), at(6, plus_rest, part), peer(1))
    cross(3)
    for (at, peer), f in zip(sides, flights):
        for n, rows in enumerate((low_rows, high_rows)):
            f["far", n].wait_recv()
            f["side_far", n, teacher_part] = send(
                at(4, rows, teacher_part), at(7, rows, teacher_part), peer(3)
            )
    for (at, peer), f in zip(sides, flights):
        for n, rows in enumerate((low_rows, high_rows)):
            f["side_far", n, student_part] = send(
                at(4, rows, student_part), at(7, rows, student_part), peer(3)
            )
    cross(4)
    for (at, peer), f in reversed(list(zip(sides, flights))):
        arrived([f["minus", 1], f["plus", 1], f["minus", 2], f["plus", 2]])
        if at is text_at:
            cross(1)
            cross(2)

    scale_t = LOG2E * TW**-0.5
    scale_s = LOG2E * SW**-0.5

    def dots(model, p, u0, count):
        rows = slice(u0 * UNIT, (u0 + count) * UNIT)
        lanes = slice(TW, W) if model else slice(0, TW)
        width = SW if model else TW
        logit, scale = ((lt, scale_t), (ls, scale_s))[model]
        logit[p, rows, :] = scale * dot_nt(
            img[u0 : u0 + count, :, lanes].reshape(count * UNIT, width),
            txt[2 * p : 2 * p + 2, :, lanes].reshape(2 * UNIT, width),
        )

    def fold(model, p, u):
        logit = (lt, ls)[model]
        rows = slice(u * UNIT, (u + 1) * UNIT)
        left, right = logit[p, rows, 0:128], logit[p, rows, 128:256]
        old = rm[model, rows, :]
        new = jnp.maximum(old, jnp.maximum(left, right))
        rm[model, rows, :] = new
        rs[model, rows, :] = (
            rs[model, rows, :] * jnp.exp2(old - new) + jnp.exp2(left - new) + jnp.exp2(right - new)
        )
        for h, part in ((0, left), (1, right)):
            lanes = slice(h * 128, h * 128 + 128)
            part = part.reshape(16, 8, 128)
            old = cm[model, p, :, lanes]
            new = jnp.maximum(old, jnp.max(part, axis=0))
            cm[model, p, :, lanes] = new
            cs[model, p, :, lanes] = cs[model, p, :, lanes] * jnp.exp2(old - new) + jnp.sum(
                jnp.exp2(part - new[None]), axis=0
            )

    def blocks(todo):
        for model, p, u0, count in todo:
            dots(model, p, u0, count)
            for u in range(u0, u0 + count):
                fold(model, p, u)

    def largest(ref, count):
        best = jnp.zeros((8, SW), F32)
        for n in range(count):
            part = jnp.abs(ref[n, :, TW:W].astype(F32)).reshape(16, 8, SW)
            best = jnp.maximum(best, jnp.max(part, axis=0))
        return jnp.broadcast_to(jnp.max(best, axis=(0, 1), keepdims=True), (1, 128))

    arrived(crossings)
    crossings.clear()
    blocks([(model, p, 0, 5) for p in range(5) for model in range(2)])

    for model, part in enumerate((teacher_part, student_part)):
        for (at, peer), f in reversed(list(zip(sides, flights))):
            for slot, names in (
                (5, (("relief", 0), ("side_minus", part))),
                (6, (("relief", 1), ("side_plus", part))),
                (7, (("side_far", 0, part), ("side_far", 1, part))),
            ):
                arrived([f[name] for name in names if model == 0 or name[0] != "relief"])
                if at is text_at:
                    cross(slot, part)
        blocks([(model, p, 5, 3) for p in range(5)])
        arrived(crossings)
        crossings.clear()
        blocks([(model, p, u0, 4) for p in range(5, 8) for u0 in (0, 4)])

    for slot, (a, r) in enumerate(SLOTS):
        for model in range(2):
            peaks = cm[model, slot]
            peak = jnp.max(peaks, axis=0, keepdims=True)
            total = jnp.sum(cs[model, slot] * jnp.exp2(peaks - peak), axis=0, keepdims=True)
            lse = log_sum(peak, total)
            for cc in range(2):
                for flip in range(4):
                    row = (((cc * 2 + a) ^ flip) * 2) + model
                    cmsg[flip, r, row : row + 1, :] = lse[:, cc * 128 : cc * 128 + 128]

    flying = [
        send(cmsg.at[cc * 2 + SLOTS[q][0]], crx.at[2 * BACK[q] + cc], t_peer(cc, q))
        for q in range(7, -1, -1)
        for cc in range(2)
        if q or cc
    ]
    for slot, (a, r) in enumerate(SLOTS):
        rows = slice(slot * UNIT, slot * UNIT + UNIT)
        for model in range(2):
            peaks = rm[model, rows, :].T
            totals = rs[model, rows, :].T
            peak = jnp.max(peaks, axis=0, keepdims=True)
            total = jnp.sum(totals * jnp.exp2(peaks - peak), axis=0, keepdims=True)
            lse = log_sum(peak, total)
            for flip in range(2):
                row = (a ^ flip) * 2 + model
                rmsg[flip, r, row : row + 1, :] = lse
    flying += [
        send(rmsg.at[SLOTS[q][0]], rrx.at[BACK[q]], i_peer(q)) for q in range(7, 0, -1)
    ]
    image_top = jnp.maximum(largest(img, NI), TINY)
    text_top = jnp.maximum(largest(txt, 2 * NP), TINY)
    top[0] = jnp.broadcast_to(image_top, (8, 128))
    top_flight = send(top.at[0], top.at[1], t_peer(1, 0))
    for b in range(NI // 2):
        turned = img[2 * b : 2 * b + 2, :, TW:W].reshape(2 * UNIT, SW).T
        ist[:, b * 512 : b * 512 + 256] = turned
        ist[:, b * 512 + 256 : b * 512 + 512] = turned
    arrived(flying)

    def combine(own, parts):
        peak = own
        for part in parts:
            peak = jnp.maximum(peak, part)
        total = jnp.exp2(own - peak)
        for part in parts:
            total = total + jnp.exp2(part - peak)
        return log_sum(peak, total)

    for r in range(4):
        rlse[r] = combine(
            rmsg[0, r], [rrx[q, (r - SLOTS[q][1]) % 4] for q in range(1, 8)]
        )
        clse[r] = combine(
            cmsg[0, r], [crx[j, (r - SLOTS[j // 2][1]) % 4] for j in range(1, 16)]
        )
    gap = (rlse[0, 1:2, :] - rlse[0, 0:1, :]) + (clse[0, 1:2, :] - clse[0, 0:1, :])

    image_code = CODE * SW**-0.5 / text_top[0:1, 0:1]
    image_flights, text_flights = [], []

    def tiles(b, p, rows_lse, diverge):
        rows = slice(b * 256, b * 256 + 256)
        a, r = SLOTS[p]
        lse_t, lse_s = rows_lse
        for h in range(2):
            lanes = slice(h * 128, h * 128 + 128)
            row = (h * 2 + a) * 2
            t = lt[p, rows, lanes]
            s = ls[p, rows, lanes]
            teacher = jnp.exp2(t - lse_t) + jnp.exp2(t - clse[r, row : row + 1, :])
            student = jnp.exp2(s - lse_s) + jnp.exp2(s - clse[r, row + 1 : row + 2, :])
            diverge = diverge + jnp.sum((teacher * (t - s)).reshape(32, 8, 128), axis=0)
            delta = student - teacher
            high = delta.astype(BF16)
            low = (delta - high.astype(F32)).astype(BF16)
            d[p, b, 0:256, lanes] = high
            d[p, b, 256:512, lanes] = low
        return diverge

    def turned_lse(b):
        found = []
        for model in range(2):
            columns = []
            for slot in (2 * b, 2 * b + 1):
                a, r = SLOTS[slot]
                row = 2 * a + model
                columns.append(jnp.broadcast_to(rlse[r, row : row + 1, :], (128, 128)).T)
            found.append(jnp.concatenate(columns, axis=0))
        return found

    FAR, NEAR = (7, 6, 5, 4), (3, 2, 1, 0)
    row_lse = {}

    def delta_tiles(b, pairs_of_text, diverge):
        if b not in row_lse:
            row_lse[b] = turned_lse(b)
        for p in pairs_of_text:
            diverge = tiles(b, p, row_lse[b], diverge)
        return diverge

    def image_dot(total, b, p):
        weights = txt[2 * p : 2 * p + 2, :, TW:W].reshape(2 * UNIT, SW)
        return total + jnp.dot(d[p, b], weights, preferred_element_type=F32)

    def image_send(total, b):
        total = total[0:256] + total[256:512]
        for h in (1, 0):
            slot = 2 * b + h
            part = total[h * 128 : h * 128 + 128]
            if slot == 0:
                out[0:UNIT] = part
            else:
                isend[slot] = encode(part * image_code)
                image_flights.append(send(isend.at[slot], irecv.at[BACK[slot]], i_peer(slot)))

    crossed = {}

    def text_part(p):
        part = jnp.dot(ist[...], d[p].reshape(2048, 256), preferred_element_type=F32)
        keep[p] = part[:, 0:128]
        xsend[p] = part[:, 128:256]

    def text_cross(p):
        crossed[p] = send(xsend.at[p], xrecv.at[p], t_peer(1, 0))

    def text_send(slot):
        crossed[slot].wait_recv()
        part = keep[slot] + xrecv[slot]
        if slot == 0:
            keep[0] = part
        else:
            tsend[slot] = encode(part * text_code)
            text_flights.append(send(tsend.at[slot], trecv.at[BACK[slot]], t_peer(0, slot)))

    diverge = jnp.zeros((8, 128), F32)
    diverge = delta_tiles(3, FAR + NEAR, diverge)
    total = jnp.zeros((512, SW), F32)
    for n, p in enumerate(FAR + NEAR):
        diverge = delta_tiles(2, (p,), diverge)
        total = image_dot(total, 3, p)
    image_send(total, 3)
    total = jnp.zeros((512, SW), F32)
    for n, p in enumerate(FAR + NEAR):
        if n < 4:
            diverge = delta_tiles(1, (p,), diverge)
            diverge = delta_tiles(0, (p,), diverge)
        total = image_dot(total, 2, p)
    image_send(total, 2)
    top_flight.wait_recv()
    chip_top = jnp.maximum(image_top, top[1, 0:1, :])
    text_code = CODE * SW**-0.5 / chip_top[0:1, 0:1]
    for some, others in ((FAR[:2], NEAR[:2]), (FAR[2:], NEAR[2:])):
        for p in others:
            diverge = delta_tiles(1, (p,), diverge)
            diverge = delta_tiles(0, (p,), diverge)
        for p in some:
            text_part(p)
        for p in some:
            text_cross(p)
    text_send(7)
    text_send(6)
    first_row = lax.broadcasted_iota(jnp.int32, (8, 128), 0) == 0
    lsend[0, 0:8] = diverge + jnp.where(first_row, jnp.broadcast_to(gap, (8, 128)), 0.0)
    lsend[0, 8:16] = jnp.broadcast_to(text_top, (8, 128))
    loss_flights = [send(lsend.at[0], lrx_i.at[BACK[q]], i_peer(q)) for q in range(7, 0, -1)]
    total = jnp.zeros((512, SW), F32)
    for p in FAR + NEAR:
        total = image_dot(total, 1, p)
    image_send(total, 1)
    text_send(5)
    text_send(4)
    total = jnp.zeros((512, SW), F32)
    for p in FAR + NEAR:
        total = image_dot(total, 0, p)
    text_part(3)
    text_part(2)
    image_send(total, 0)
    text_cross(3)
    text_cross(2)
    text_part(1)
    text_part(0)
    text_cross(1)
    text_cross(0)
    for slot in NEAR:
        text_send(slot)

    arrived(loss_flights)
    loss_part = lsend[0, 0:8]
    for q in range(1, 8):
        loss_part = loss_part + lrx_i[q, 0:8]
    lsend[1, 0:8] = loss_part
    lsend[1, 8:16] = jnp.broadcast_to(chip_top, (8, 128))
    loss_flights = [
        send(lsend.at[1], lrx_t.at[2 * BACK[j // 2] + j % 2], t_peer(j % 2, j // 2))
        for j in range(15, 0, -1)
    ]

    image_total = out[0:UNIT] * SW**-0.5
    for q, flight in zip([BACK[q] for q in (7, 6, 5, 4, 3, 2, 1)], image_flights):
        flight.wait_recv()
        image_total = image_total + decode(irecv[q]) * (lrx_i[q, 8:9, 0:1] * (1.0 / CODE))
    out[0:UNIT] = image_total
    arrived(loss_flights)
    loss_part = lsend[1, 0:8]
    for q in range(1, 16):
        loss_part = loss_part + lrx_t[q, 0:8]
    loss = jnp.sum(loss_part, axis=(0, 1), keepdims=True) * (LN2 / (2.0 * pairs))
    out[2 * UNIT : 2 * UNIT + 8] = jnp.broadcast_to(loss, (8, SW))
    text_total = keep[0] * SW**-0.5
    for q, flight in zip([BACK[q] for q in (7, 6, 5, 4, 3, 2, 1)], text_flights):
        flight.wait_recv()
        text_total = text_total + decode(trecv[q]) * (lrx_t[2 * q, 8:9, 0:1] * (1.0 / CODE))
    out[UNIT : 2 * UNIT] = text_total.T
    for copy in begun:
        copy.wait_send()


def local(teacher_image, teacher_text, student_image, student_text):
    pairs = teacher_image.shape[0] * lax.axis_size("img") * lax.axis_size("txt")
    vmem = pltpu.VMEM
    result = pl.pallas_call(
        functools.partial(kernel, pairs),
        out_shape=jax.ShapeDtypeStruct((2 * UNIT + 8, SW), F32),
        in_specs=[pl.BlockSpec(memory_space=pl.ANY)] * 4,
        out_specs=pl.BlockSpec(memory_space=vmem),
        scratch_shapes=[
            vmem((NI, UNIT, W), BF16),
            vmem((2 * NP, UNIT, W), BF16),
            vmem((NP, NI * UNIT, 256), F32),
            vmem((NP, NI * UNIT, 256), F32),
            vmem((2, NI * UNIT, 128), F32),
            vmem((2, NI * UNIT, 128), F32),
            vmem((2, NP, 8, 256), F32),
            vmem((2, NP, 8, 256), F32),
            vmem((NP, NI // 2, 512, 256), BF16),
            vmem((SW, 2 * NI * UNIT), BF16),
            vmem((2, 4, 8, 128), F32),
            vmem((4, 4, 8, 128), F32),
            vmem((8, 4, 8, 128), F32),
            vmem((16, 4, 8, 128), F32),
            vmem((4, 8, 128), F32),
            vmem((4, 8, 128), F32),
            vmem((8, UNIT, SW), BF16),
            vmem((8, UNIT, SW), BF16),
            vmem((8, SW, UNIT), F32),
            vmem((8, SW, UNIT), F32),
            vmem((8, SW, UNIT), F32),
            vmem((8, SW, UNIT), BF16),
            vmem((8, SW, UNIT), BF16),
            vmem((2, 16, 128), F32),
            vmem((8, 16, 128), F32),
            vmem((16, 16, 128), F32),
            vmem((2, 8, 128), F32),
            pltpu.SemaphoreType.DMA((4,)),
            pltpu.SemaphoreType.DMA((128,)),
            pltpu.SemaphoreType.DMA((128,)),
        ],
        compiler_params=pltpu.CompilerParams(
            collective_id=0, has_side_effects=True, vmem_limit_bytes=62 * 2**20
        ),
        cost_estimate=pl.CostEstimate(
            flops=16_000_000_000, bytes_accessed=1_500_000, transcendentals=20_000_000
        ),
    )(teacher_image, teacher_text, student_image, student_text)
    return result[2 * UNIT, 0], result[0:UNIT], result[UNIT : 2 * UNIT]


def solution(mesh):
    in_specs = (
        P(("img", "txt"), None),
        P(("txt", "img"), None),
        P(("img", "txt"), None),
        P(("txt", "img"), None),
    )
    out_specs = (P(), P(("img", "txt"), None), P(("txt", "img"), None))
    return jax.shard_map(local, mesh=mesh, in_specs=in_specs, out_specs=out_specs, check_vma=False)
```
